32 devices in a mesh: grp: 2 (over y), ctx: 8 (over z, x), tp: 2 (over core).
Axes of the slice: x: 2, y: 2, z: 4, core: 2. Of those that a mesh axis runs over, the one named last changes fastest.
Arguments:
- queries: bfloat16 [2048, 4096], P(('grp', 'ctx'), 'tp'), parts along dimension 0, may hold values from -6 to 6
- key_proj: bfloat16 [2048, 4096], P(('grp', 'ctx'), 'tp'), parts along dimension 0, may hold values from -6 to 6
- value_proj: bfloat16 [2048, 4096], P(('grp', 'ctx'), 'tp'), parts along dimension 0, may hold values from -6 to 6
- out_grad: bfloat16 [2048, 4096], P(('grp', 'ctx', 'tp')), parts along dimension 0, may hold values from -23 to 23
- filter_taps: bfloat16 [128, 4096], P(None, 'tp'), may hold values from -0.5 to 0.5
Outputs:
- query_grad: bfloat16 [2048, 4096], P(('grp', 'ctx'), 'tp'), parts along dimension 0
- key_grad: bfloat16 [2048, 4096], P(('grp', 'ctx'), 'tp'), parts along dimension 0
- value_grad: bfloat16 [2048, 4096], P(('grp', 'ctx'), 'tp'), parts along dimension 0
- filter_grad: bfloat16 [128, 8192], P(None, ('grp', 'tp')), parts along dimension 1
The draws below stay inside these ranges and needn't reach their ends.
There are 2 independent parts, one for each index of `grp`. The reference program is written for one: setup_inputs(seed, part) draws one part's arguments, and reference() takes and returns one part's arrays. A program takes and returns all parts, laid end to end along the dimension named above; an argument that names none is the same for every part. Nothing has to cross between parts.
All inputs are finite; a program needn't handle non-finite values.
Results may differ from the reference program's by a relative error of at most 0.0057.
Values may be sent and summed in bfloat16 or wider, within the bound.
A program may use at most 64 MiB of HBM per device.

```python
import math
import jax
import jax.numpy as jnp
from jax import lax

D = 4096
TAPS = 128
TOKENS = 1024


def draw_out_grad(key, part):
    first, second = jax.random.split(key, 2)
    noise = jax.random.truncated_normal(first, -4.0, 4.0, (TOKENS, D), jnp.float32)
    row_scale = jnp.exp(jax.random.uniform(second, (TOKENS, 1), jnp.float32, math.log(0.32), math.log(3.2)))
    position = jnp.arange(TOKENS, dtype=jnp.float32)[:, None] / float(TOKENS - 1)
    envelope = jnp.exp(math.log(3.0) * position - 0.5 * math.log(3.0))
    return (noise * row_scale * envelope).astype(jnp.bfloat16)


def levels(rng, dims, shards, low, top_value):
    def one(axis_at, blocks):
        heights = jax.random.uniform(jax.random.fold_in(jax.random.fold_in(rng, 6), axis_at), (blocks,), jnp.float32, low / len(shards), top_value / len(shards))
        return jnp.repeat(jnp.exp(heights), dims[axis_at] // blocks).reshape((-1,) + (1,) * (len(dims) - axis_at - 1))

    factor_of = one(*shards[0])
    for cut in shards[1:]:
        factor_of = factor_of * one(*cut)
    return factor_of


def scatter_about(stream_key, dims, scale, most, pieces=(), kind=jnp.bfloat16):
    loudness = levels(stream_key, dims, pieces, -0.22, 0.18) if pieces else 1.0
    result = jax.random.normal(stream_key, dims, jnp.float32) * scale * loudness
    return jnp.minimum(jnp.maximum(result, -most), most).astype(kind)


def setup_inputs(seed: int = 0, part: int = 0) -> dict:
    seeds = jax.random.split(jax.random.key(seed), 6)
    part_splits = jax.random.split(jax.random.fold_in(seeds[5], part), 6)
    queries = scatter_about(part_splits[0], (TOKENS, D), 1.0, 6.0, ((0, 8), (1, 2)))
    key_proj = scatter_about(part_splits[1], (TOKENS, D), 1.0, 6.0, ((0, 8), (1, 2)))
    value_proj = scatter_about(part_splits[2], (TOKENS, D), 1.0, 6.0, ((0, 8), (1, 2)))
    out_grad = draw_out_grad(jax.random.fold_in(jax.random.fold_in(seeds[5], part), 71), part)
    filter_taps = scatter_about(seeds[4], (TAPS, D), TAPS ** -0.5, 0.5, ((1, 2),))
    return dict(queries=queries, key_proj=key_proj, value_proj=value_proj, out_grad=out_grad, filter_taps=filter_taps)


def reference(queries, key_proj, value_proj, out_grad, filter_taps):
    margin = TAPS - 1
    product = (key_proj.astype(jnp.float32) * value_proj.astype(jnp.float32)).astype(jnp.bfloat16)
    gated = (out_grad.astype(jnp.float32) * queries.astype(jnp.float32)).astype(jnp.bfloat16)
    padded_kv = jnp.concatenate([jnp.zeros((margin, D), jnp.bfloat16), product], axis=0)
    padded_gate = jnp.concatenate([gated, jnp.zeros((margin, D), jnp.bfloat16)], axis=0)
    weights = filter_taps.astype(jnp.float32)
    gate_f = gated.astype(jnp.float32)

    def stepper(carry, index):
        mixture, spread = carry
        earlier = lax.dynamic_slice_in_dim(padded_kv, (margin - index).astype(jnp.int32), TOKENS, 0).astype(jnp.float32)
        later = lax.dynamic_slice_in_dim(padded_gate, index.astype(jnp.int32), TOKENS, 0).astype(jnp.float32)
        coeff = lax.dynamic_index_in_dim(weights, index.astype(jnp.int32), 0, keepdims=False)
        mixture = mixture + coeff * earlier
        spread = spread + coeff * later
        tap_row = lax.optimization_barrier(jnp.sum(gate_f * earlier, axis=0))
        return ((mixture, spread), tap_row)
    initial = (jnp.zeros((TOKENS, D), jnp.float32), jnp.zeros((TOKENS, D), jnp.float32))
    (mixture, spread), tap_rows = lax.scan(stepper, initial, jnp.arange(TAPS, dtype=jnp.int32))
    query_grad = (out_grad.astype(jnp.float32) * mixture).astype(jnp.bfloat16)
    key_grad = (spread * value_proj.astype(jnp.float32)).astype(jnp.bfloat16)
    value_grad = (spread * key_proj.astype(jnp.float32)).astype(jnp.bfloat16)
    filter_grad = (tap_rows * (1.0 / math.sqrt(TOKENS))).astype(jnp.bfloat16)
    return (query_grad, key_grad, value_grad, filter_grad)
```

```python
import functools
import math

import jax
import jax.numpy as jnp
import ml_dtypes
import numpy as np
from jax import lax
from jax.experimental import pallas as pl
from jax.experimental.pallas import tpu as pltpu
from jax.sharding import PartitionSpec as P

MESH = pl.DeviceIdType.MESH
F32 = jnp.float32
BF16 = jnp.bfloat16
WIDTH = 512
DIRECT_PEERS = 8


def split(matrix):
    high = matrix.astype(ml_dtypes.bfloat16)
    low = (matrix - high.astype(np.float64)).astype(ml_dtypes.bfloat16)
    return np.concatenate([high, low], axis=0)


def transforms(length):
    half = length // 2
    turns = (2 * np.arange(half)[:, None] + 1) * np.arange(length)[None, :] % (2 * length)
    angle = np.pi * turns / length
    forward = np.concatenate([np.cos(angle), -np.sin(angle)], axis=0)
    inverse = forward.T / half
    return split(forward), split(inverse[:half]), split(inverse[half:])


def spectrum(matrix, rows):
    both = jnp.dot(matrix, rows, preferred_element_type=F32)
    half = both.shape[0] // 2
    return both[:half] + both[half:]


def restore(matrix, freqs):
    half = matrix.shape[0] // 2
    high = freqs.astype(BF16)
    low = (freqs - high.astype(F32)).astype(BF16)
    both = jnp.dot(matrix, high, preferred_element_type=F32)
    extra = jnp.dot(matrix[:half], low, preferred_element_type=F32)
    return both[:half] + both[half:] + extra


def times(a, b):
    half = a.shape[0] // 2
    ar, ai, br, bi = a[:half], a[half:], b[:half], b[half:]
    return jnp.concatenate([ar * br - ai * bi, ar * bi + ai * br], axis=0)


def times_conj(a, b):
    half = a.shape[0] // 2
    ar, ai, br, bi = a[:half], a[half:], b[:half], b[half:]
    return jnp.concatenate([ar * br + ai * bi, ai * br - ar * bi], axis=0)


def kernel(
    peers, direct, scale,
    q_ref, k_ref, v_ref, og_ref, h_ref, fwd_ref, inv0_ref, inv1_ref,
    dq_ref, dk_ref, dv_ref, df_ref,
    up, prod, gate, before, after, part, parts_in, hspec,
    up_sems, halo_send, halo_recv, rs_send, rs_recv, ag_send, ag_recv,
):
    grp, me, core = (lax.axis_index(a) for a in ("grp", "ctx", "tp"))
    rows, channels = q_ref.shape
    taps = h_ref.shape[0]
    chunks = channels // WIDTH
    mine = rows // 2
    has_before, has_after = me > 0, me < peers - 1

    def at(other):
        return (grp, other, core)

    barrier = pltpu.get_barrier_semaphore()
    pl.semaphore_signal(barrier, inc=1, device_id=(grp, me, 1 - core), device_id_type=MESH)
    if direct:
        for step in range(1, peers):
            pl.semaphore_signal(
                barrier, inc=1, device_id=at(lax.rem(me + step, peers)), device_id_type=MESH
            )
        pl.semaphore_wait(barrier, peers)
    else:
        for step in (1, peers - 1):
            pl.semaphore_signal(
                barrier, inc=1, device_id=at(lax.rem(me + step, peers)), device_id_type=MESH
            )
        pl.semaphore_wait(barrier, 3)

    def columns(index):
        return pl.ds(pl.multiple_of(index * WIDTH, WIDTH), WIDTH)

    def up_copies():
        own = up.at[pl.ds(pl.multiple_of(core * mine, mine), mine)]
        near = og_ref.at[:, pl.ds(pl.multiple_of(core * channels, channels), channels)]
        far = og_ref.at[:, pl.ds(pl.multiple_of((1 - core) * channels, channels), channels)]
        local = pltpu.make_async_copy(near, own, up_sems.at[0])
        remote = pltpu.make_async_remote_copy(
            src_ref=far, dst_ref=own, send_sem=up_sems.at[1], recv_sem=up_sems.at[2],
            device_id=(grp, me, 1 - core), device_id_type=MESH,
        )
        return local, remote

    def upward(index):
        return pltpu.make_async_remote_copy(
            src_ref=prod.at[index], dst_ref=before.at[index],
            send_sem=halo_send.at[0, index], recv_sem=halo_recv.at[0, index],
            device_id=at(lax.rem(me + 1, peers)), device_id_type=MESH,
        )

    def downward(index):
        return pltpu.make_async_remote_copy(
            src_ref=gate.at[index], dst_ref=after.at[index],
            send_sem=halo_send.at[1, index], recv_sem=halo_recv.at[1, index],
            device_id=at(lax.rem(me + peers - 1, peers)), device_id_type=MESH,
        )

    for copy in up_copies():
        copy.start()

    @pl.loop(0, chunks)
    def _(index):
        cols = columns(index)
        prod[index] = (k_ref[:, cols].astype(F32) * v_ref[:, cols].astype(F32)).astype(BF16)

        @pl.when(has_after)
        def _():
            upward(index).start()

    for copy in up_copies():
        copy.wait()

    @pl.loop(0, chunks)
    def _(index):
        cols = columns(index)
        gate[index] = (up[:, cols].astype(F32) * q_ref[:, cols].astype(F32)).astype(BF16)

        @pl.when(has_before)
        def _():
            downward(index).start()

        @pl.when(jnp.logical_not(has_before))
        def _():
            before[index] = jnp.zeros((rows, WIDTH), BF16)

        @pl.when(jnp.logical_not(has_after))
        def _():
            after[index] = jnp.zeros((rows, WIDTH), BF16)

        hspec[index] = spectrum(fwd_ref[:, :taps], h_ref[:, cols])

    share = taps // peers if direct else taps

    def scatter(step, index):
        owner = lax.rem(me + step, peers)
        return pltpu.make_async_remote_copy(
            src_ref=part.at[index, pl.ds(pl.multiple_of(owner * share, share), share)],
            dst_ref=parts_in.at[step - 1, index],
            send_sem=rs_send.at[step - 1, index], recv_sem=rs_recv.at[step - 1, index],
            device_id=at(owner), device_id_type=MESH,
        )

    def collect(step, index):
        block = df_ref.at[pl.ds(pl.multiple_of(me * share, share), share), columns(index)]
        return pltpu.make_async_remote_copy(
            src_ref=block, dst_ref=block,
            send_sem=ag_send.at[step - 1, index], recv_sem=ag_recv.at[step - 1, index],
            device_id=at(lax.rem(me + step, peers)), device_id_type=MESH,
        )

    @pl.loop(0, chunks)
    def _(index):
        cols = columns(index)

        @pl.when(has_before)
        def _():
            upward(index).wait_recv()

        pspec = spectrum(fwd_ref[...], jnp.concatenate([before[index], prod[index]], axis=0))
        gspec = spectrum(fwd_ref[:, rows:], gate[index])
        terms = restore(inv0_ref[...], times_conj(gspec, pspec))
        if direct:
            part[index] = terms.astype(BF16)
            for step in range(1, peers):
                scatter(step, index).start()
        else:
            df_ref[:, cols] = terms
        mixture = restore(inv1_ref[...], times(pspec, hspec[index]))
        dq_ref[:, cols] = (up[:, cols].astype(F32) * mixture).astype(BF16)

    @pl.loop(0, chunks)
    def _(index):
        cols = columns(index)

        @pl.when(has_after)
        def _():
            downward(index).wait_recv()

        gspec = spectrum(fwd_ref[...], jnp.concatenate([gate[index], after[index]], axis=0))
        spread = restore(inv0_ref[...], times_conj(gspec, hspec[index]))
        dk_ref[:, cols] = (spread * v_ref[:, cols].astype(F32)).astype(BF16)
        dv_ref[:, cols] = (spread * k_ref[:, cols].astype(F32)).astype(BF16)

    if direct:

        @pl.loop(0, chunks)
        def _(index):
            own = pl.ds(pl.multiple_of(me * share, share), share)
            total = part[index, own].astype(F32)
            for step in range(1, peers):
                scatter(step, index).wait_recv()
                total = total + parts_in[step - 1, index].astype(F32)
            df_ref[own, columns(index)] = (total * scale).astype(BF16)
            for step in range(1, peers):
                collect(step, index).start()

    @pl.loop(0, chunks)
    def _(index):
        @pl.when(has_after)
        def _():
            upward(index).wait_send()

        @pl.when(has_before)
        def _():
            downward(index).wait_send()

        if direct:
            for step in range(1, peers):
                scatter(step, index).wait_send()
            for step in range(1, peers):
                collect(step, index).wait()


def local(queries, key_proj, value_proj, out_grad, filter_taps):
    rows, channels = queries.shape
    taps = filter_taps.shape[0]
    peers = lax.axis_size("ctx")
    direct = peers <= DIRECT_PEERS
    scale = 1.0 / math.sqrt(peers * rows)
    chunks = channels // WIDTH
    matrices = [jnp.asarray(m) for m in transforms(2 * rows)]
    steps = peers - 1 if direct else 1
    share = taps // peers if direct else 16
    like = jax.ShapeDtypeStruct((rows, channels), BF16)
    vmem = pl.BlockSpec(memory_space=pltpu.VMEM)
    tile = (chunks, rows, WIDTH)
    dma = pltpu.SemaphoreType.DMA
    query_grad, key_grad, value_grad, filter_grad = pl.pallas_call(
        functools.partial(kernel, peers, direct, scale),
        name="hyena_backward",
        out_shape=[like, like, like,
                   jax.ShapeDtypeStruct((taps, channels), BF16 if direct else F32)],
        in_specs=[vmem, vmem, vmem, pl.BlockSpec(memory_space=pl.ANY)] + [vmem] * 4,
        out_specs=[vmem] * 4,
        scratch_shapes=[
            pltpu.VMEM((rows, channels), BF16),
            pltpu.VMEM(tile, BF16),
            pltpu.VMEM(tile, BF16),
            pltpu.VMEM(tile, BF16),
            pltpu.VMEM(tile, BF16),
            pltpu.VMEM((chunks, taps, WIDTH), BF16),
            pltpu.VMEM((steps, chunks, share, WIDTH), BF16),
            pltpu.VMEM((chunks, 2 * rows, WIDTH), F32),
            dma((3,)), dma((2, chunks)), dma((2, chunks)),
            dma((steps, chunks)), dma((steps, chunks)), dma((steps, chunks)), dma((steps, chunks)),
        ],
        compiler_params=pltpu.CompilerParams(
            collective_id=0, has_side_effects=True, vmem_limit_bytes=40 * 1024 * 1024
        ),
        cost_estimate=pl.CostEstimate(
            flops=20 * rows * rows * channels, bytes_accessed=18 * rows * channels,
            transcendentals=0,
        ),
    )(queries, key_proj, value_proj, out_grad, filter_taps, *matrices)
    if not direct:
        filter_grad = (lax.psum(filter_grad, "ctx") * scale).astype(BF16)
    return query_grad, key_grad, value_grad, filter_grad


def solution(mesh):
    tokens = P(("grp", "ctx"), "tp")
    return jax.shard_map(
        local,
        mesh=mesh,
        in_specs=(tokens, tokens, tokens, P(("grp", "ctx", "tp"), None), P(None, "tp")),
        out_specs=(tokens, tokens, tokens, P(None, ("grp", "tp"))),
        check_vma=False,
    )
```

```python
import functools
import math

import jax
import jax.numpy as jnp
import ml_dtypes
import numpy as np
from jax import lax
from jax.experimental import pallas as pl
from jax.experimental.pallas import tpu as pltpu
from jax.sharding import PartitionSpec as P

MESH = pl.DeviceIdType.MESH
F32 = jnp.float32
BF16 = jnp.bfloat16
WIDTH = 512
CUTS = 4
VMEM_LIMIT = 60 * 1024 * 1024
DIRECT_PEERS = 8
PLAN = (
    "g0 g1 g2 g3 h0 h1 h2 h3 C0 C1 s0 C2 s1 L0 C3 s2 s3 L1 P0 L2 P1 L3 P2 F0 P3 F1 D0 F2 D1 F3 D2 D3"
)


def split(matrix):
    high = matrix.astype(ml_dtypes.bfloat16)
    low = (matrix - high.astype(np.float64)).astype(ml_dtypes.bfloat16)
    return np.concatenate([high, low], axis=0)


def transforms(length):
    half = length // 2
    turns = (2 * np.arange(half)[:, None] + 1) * np.arange(length)[None, :] % (2 * length)
    angle = np.pi * turns / length
    forward = np.concatenate([np.cos(angle), -np.sin(angle)], axis=0)
    inverse = forward.T / half
    return split(forward), split(inverse[:half]), split(inverse[half:])


def spectrum(matrix, rows):
    both = jnp.dot(matrix, rows, preferred_element_type=F32)
    half = both.shape[0] // 2
    return both[:half] + both[half:]


def restore(matrix, freqs):
    half = matrix.shape[0] // 2
    high = freqs.astype(BF16)
    low = (freqs - high.astype(F32)).astype(BF16)
    both = jnp.dot(matrix, high, preferred_element_type=F32)
    extra = jnp.dot(matrix[:half], low, preferred_element_type=F32)
    return both[:half] + both[half:] + extra


def times(a, b):
    half = a.shape[0] // 2
    ar, ai, br, bi = a[:half], a[half:], b[:half], b[half:]
    return jnp.concatenate([ar * br - ai * bi, ar * bi + ai * br], axis=0)


def times_conj(a, b):
    half = a.shape[0] // 2
    ar, ai, br, bi = a[:half], a[half:], b[:half], b[half:]
    return jnp.concatenate([ar * br + ai * bi, ai * br - ar * bi], axis=0)


def kernel(
    peers, direct, scale,
    q_hbm, k_hbm, v_hbm, og_hbm, h_hbm, fwd_hbm, inv0_hbm, inv1_hbm,
    dq_hbm, dk_hbm, dv_hbm, df_hbm,
    dq_ref, dk_ref, dv_ref, df_ref, q_ref, k_ref, v_ref, h_ref, fwd_ref, inv0_ref, inv1_ref,
    up, prod, gate, before, after, part, lane_in, pair_in, pair_out, hspec,
    kv_sems, in_sems, up_sems, halo_send, halo_recv,
    lane_send, lane_recv, pair_send, pair_recv, ag_send, ag_recv, fw_send, fw_recv, out_sems,
):
    grp, me, core = (lax.axis_index(a) for a in ("grp", "ctx", "tp"))
    rows, channels = q_ref.shape
    taps = h_ref.shape[0]
    chunks = channels // WIDTH
    mine = rows // 2
    has_before, has_after = me > 0, me < peers - 1
    lanes = max(peers // 2, 1)
    place, side = me // 2, lax.rem(me, 2)
    twin = 2 * place + 1 - side

    def at(other):
        return (grp, other, core)

    def lane(step):
        return 2 * lax.rem(place + step, lanes) + side

    after_me, before_me = lax.rem(me + 1, peers), lax.rem(me + peers - 1, peers)
    barrier = pltpu.get_barrier_semaphore()
    greeted = [(grp, me, 1 - core), at(after_me), at(before_me)]
    if direct:
        greeted += [at(lane(step)) for step in range(1, lanes)]
    for device in greeted:
        pl.semaphore_signal(barrier, inc=1, device_id=device, device_id_type=MESH)

    def columns(index):
        return pl.ds(index * WIDTH, WIDTH)

    kv_loads = []
    for index in range(chunks):
        cols = columns(index)
        kv_loads.append([
            pltpu.make_async_copy(hbm.at[:, cols], ref.at[:, cols], kv_sems.at[number, index])
            for number, (hbm, ref) in enumerate([(k_hbm, k_ref), (v_hbm, v_ref)])
        ])
        for copy in kv_loads[-1]:
            copy.start()
    own_rows = up.at[pl.ds(pl.multiple_of(core * mine, mine), mine)]
    near = og_hbm.at[:, pl.ds(pl.multiple_of(core * channels, channels), channels)]
    far = og_hbm.at[:, pl.ds(pl.multiple_of((1 - core) * channels, channels), channels)]
    others = [(q_hbm, q_ref), (h_hbm, h_ref), (fwd_hbm, fwd_ref), (inv0_hbm, inv0_ref),
              (inv1_hbm, inv1_ref), (near, own_rows)]
    loads = [pltpu.make_async_copy(hbm, ref, in_sems.at[number])
             for number, (hbm, ref) in enumerate(others)]
    for copy in loads:
        copy.start()

    up_copy = pltpu.make_async_remote_copy(
        src_ref=far, dst_ref=own_rows, send_sem=up_sems.at[0], recv_sem=up_sems.at[1],
        device_id=(grp, me, 1 - core), device_id_type=MESH,
    )

    def upward(index):
        return pltpu.make_async_remote_copy(
            src_ref=prod.at[index], dst_ref=before.at[index],
            send_sem=halo_send.at[0, index], recv_sem=halo_recv.at[0, index],
            device_id=at(after_me), device_id_type=MESH,
        )

    def downward(index):
        return pltpu.make_async_remote_copy(
            src_ref=gate.at[index], dst_ref=after.at[index],
            send_sem=halo_send.at[1, index], recv_sem=halo_recv.at[1, index],
            device_id=at(before_me), device_id_type=MESH,
        )

    share = taps // lanes if direct else taps
    piece = share // 2

    def scatter(step, index):
        owner = lax.rem(place + step, lanes)
        return pltpu.make_async_remote_copy(
            src_ref=part.at[index, pl.ds(pl.multiple_of(owner * share, share), share)],
            dst_ref=lane_in.at[step - 1, index],
            send_sem=lane_send.at[step - 1, index], recv_sem=lane_recv.at[step - 1, index],
            device_id=at(lane(step)), device_id_type=MESH,
        )

    def swap(index):
        return pltpu.make_async_remote_copy(
            src_ref=pair_out.at[index], dst_ref=pair_in.at[index],
            send_sem=pair_send.at[index], recv_sem=pair_recv.at[index],
            device_id=at(twin), device_id_type=MESH,
        )

    def block(step, index):
        holder = lax.rem(place + lanes - step, lanes)
        start = pl.multiple_of(holder * share + side * piece, piece)
        return df_ref.at[pl.ds(start, piece), columns(index)]

    def collect(step, index):
        return pltpu.make_async_remote_copy(
            src_ref=block(0, index), dst_ref=block(0, index),
            send_sem=ag_send.at[step - 1, index], recv_sem=ag_recv.at[step - 1, index],
            device_id=at(lane(step)), device_id_type=MESH,
        )

    def forward(step, index):
        return pltpu.make_async_remote_copy(
            src_ref=block(step, index), dst_ref=block(step, index),
            send_sem=fw_send.at[step, index], recv_sem=fw_recv.at[step, index],
            device_id=at(twin), device_id_type=MESH,
        )

    def store(number, index):
        ref = (dq_ref, dk_ref, dv_ref, df_ref)[number]
        hbm = (dq_hbm, dk_hbm, dv_hbm, df_hbm)[number]
        cols = columns(index)
        return pltpu.make_async_copy(ref.at[:, cols], hbm.at[:, cols], out_sems.at[number, index])

    def make_product(index):
        cols = columns(index)
        for copy in kv_loads[index]:
            copy.wait()
        prod[index] = (k_ref[:, cols].astype(F32) * v_ref[:, cols].astype(F32)).astype(BF16)

    make_product(0)
    pl.semaphore_wait(barrier, len(greeted))
    up_copy.start()
    for index in range(chunks):
        if index:
            make_product(index)

        @pl.when(has_after)
        def _():
            upward(index).start()

    for copy in loads:
        copy.wait()
    up_copy.wait()

    @pl.when(jnp.logical_not(has_before))
    def _():
        before[...] = jnp.zeros_like(before)

    @pl.when(jnp.logical_not(has_after))
    def _():
        after[...] = jnp.zeros_like(after)

    def make_gate(index):
        cols = columns(index)
        gate[index] = (up[:, cols].astype(F32) * q_ref[:, cols].astype(F32)).astype(BF16)

    def send_gate(index):
        @pl.when(has_before)
        def _():
            downward(index).start()

    def first(index):
        cols = columns(index)

        @pl.when(has_before)
        def _():
            upward(index).wait_recv()

        pspec = spectrum(fwd_ref[...], jnp.concatenate([before[index], prod[index]], axis=0))
        gspec = spectrum(fwd_ref[:, rows:], gate[index])
        terms = restore(inv0_ref[...], times_conj(gspec, pspec))
        if direct:
            part[index] = terms.astype(BF16)
            for step in range(1, lanes):
                scatter(step, index).start()
        else:
            df_ref[:, cols] = terms
            store(3, index).start()
        mixture = restore(inv1_ref[...], times(pspec, hspec[index]))
        dq_ref[:, cols] = (up[:, cols].astype(F32) * mixture).astype(BF16)
        store(0, index).start()

    def second(index):
        cols = columns(index)

        @pl.when(has_after)
        def _():
            downward(index).wait_recv()

        gspec = spectrum(fwd_ref[...], jnp.concatenate([gate[index], after[index]], axis=0))
        spread = restore(inv0_ref[...], times_conj(gspec, hspec[index]))
        dk_ref[:, cols] = (spread * v_ref[:, cols].astype(F32)).astype(BF16)
        dv_ref[:, cols] = (spread * k_ref[:, cols].astype(F32)).astype(BF16)
        store(1, index).start()
        store(2, index).start()

    def lane_total(index, which):
        start = pl.multiple_of(place * share + which * piece, piece)
        total = part[index, pl.ds(start, piece)].astype(F32)
        within = pl.ds(pl.multiple_of(which * piece, piece), piece)
        for step in range(1, lanes):
            total = total + lane_in[step - 1, index, within].astype(F32)
        return total

    def reduce_lane(index):
        for step in range(1, lanes):
            scatter(step, index).wait_recv()
        pair_out[index] = lane_total(index, 1 - side).astype(BF16)
        swap(index).start()

    def reduce_pair(index):
        swap(index).wait_recv()
        total = lane_total(index, side) + pair_in[index].astype(F32)
        block(0, index)[...] = (total * scale).astype(BF16)
        for step in range(1, lanes):
            collect(step, index).start()
        forward(0, index).start()

    def pass_on(index):
        for step in range(1, lanes):
            collect(step, index).wait_recv()
            forward(step, index).start()

    def taps_spectrum(index):
        hspec[index] = spectrum(fwd_ref[:, :taps], h_ref[:, columns(index)])

    run = dict(g=make_gate, s=send_gate, h=taps_spectrum, C=first, D=second)
    if direct:
        run.update(L=reduce_lane, P=reduce_pair, F=pass_on)
    for entry in PLAN.split():
        if entry[0] in run:
            run[entry[0]](int(entry[1]))

    for index in range(chunks):
        @pl.when(has_after)
        def _():
            upward(index).wait_send()

        @pl.when(has_before)
        def _():
            downward(index).wait_send()

        if direct:
            for step in range(1, lanes):
                scatter(step, index).wait_send()
                collect(step, index).wait_send()
            swap(index).wait_send()
            for step in range(lanes):
                forward(step, index).wait()
            store(3, index).start()
    for index in range(chunks):
        for number in range(4):
            store(number, index).wait()


def deliver(*refs):
    count = len(refs) // 3
    sources, targets, held, sems = refs[:count], refs[count:2 * count], refs[2 * count:-1], refs[-1]
    loads, stores = [], []
    for i in range(count):
        rows = sources[i].shape[0] // CUTS
        for j in range(CUTS):
            part = pl.ds(j * rows, rows)
            here = held[i].at[part]
            loads.append(pltpu.make_async_copy(sources[i].at[part], here, sems.at[0, i, j]))
            stores.append(pltpu.make_async_copy(here, targets[i].at[part], sems.at[1, i, j]))
    for load in loads:
        load.start()
    for load, store in zip(loads, stores):
        load.wait()
        store.start()
    for store in stores:
        store.wait()


def local(queries, key_proj, value_proj, out_grad, filter_taps):
    rows, channels = queries.shape
    taps = filter_taps.shape[0]
    peers = lax.axis_size("ctx")
    direct = peers == DIRECT_PEERS
    scale = 1.0 / math.sqrt(peers * rows)
    chunks = channels // WIDTH
    matrices = [jnp.asarray(m) for m in transforms(2 * rows)]
    lanes = peers // 2 if direct else 2
    share = taps // lanes if direct else 32
    like = jax.ShapeDtypeStruct((rows, channels), BF16)
    hbm = pl.BlockSpec(memory_space=pltpu.HBM)
    tile = (chunks, rows, WIDTH)
    dma = pltpu.SemaphoreType.DMA
    whole = [pltpu.VMEM(x.shape, BF16)
             for x in (queries, key_proj, value_proj, filter_taps, *matrices)]
    results = pl.pallas_call(
        functools.partial(kernel, peers, direct, scale),
        name="hyena_backward",
        out_shape=[like, like, like,
                   jax.ShapeDtypeStruct((taps, channels), BF16 if direct else F32)],
        in_specs=[hbm] * 8,
        out_specs=[hbm] * 4,
        scratch_shapes=[pltpu.VMEM((rows, channels), BF16)] * 3
        + [pltpu.VMEM((taps, channels), BF16 if direct else F32)] + whole + [pltpu.VMEM((rows, channels), BF16)]
        + [pltpu.VMEM(tile, BF16)] * 4 + [
            pltpu.VMEM((chunks, taps, WIDTH), BF16),
            pltpu.VMEM((lanes - 1, chunks, share, WIDTH), BF16),
            pltpu.VMEM((chunks, share // 2, WIDTH), BF16),
            pltpu.VMEM((chunks, share // 2, WIDTH), BF16),
            pltpu.VMEM((chunks, 2 * rows, WIDTH), F32),
            dma((2, chunks)), dma((6,)), dma((2,)), dma((2, chunks)), dma((2, chunks)),
            dma((lanes - 1, chunks)), dma((lanes - 1, chunks)), dma((chunks,)), dma((chunks,)),
            dma((lanes - 1, chunks)), dma((lanes - 1, chunks)),
            dma((lanes, chunks)), dma((lanes, chunks)), dma((4, chunks)),
        ],
        compiler_params=pltpu.CompilerParams(
            collective_id=0, has_side_effects=True, vmem_limit_bytes=VMEM_LIMIT
        ),
        cost_estimate=pl.CostEstimate(
            flops=20 * rows * rows * channels, bytes_accessed=18 * rows * channels,
            transcendentals=0,
        ),
    )(queries, key_proj, value_proj, out_grad, filter_taps, *matrices)
    results = list(results)
    if not direct:
        results[3] = (lax.psum(results[3], "ctx") * scale).astype(BF16)
    return tuple(pl.pallas_call(
        deliver,
        name="deliver",
        out_shape=[jax.ShapeDtypeStruct(x.shape, x.dtype) for x in results],
        in_specs=[hbm] * 4,
        out_specs=[hbm] * 4,
        scratch_shapes=[pltpu.VMEM(x.shape, x.dtype) for x in results] + [dma((2, 4, CUTS))],
        compiler_params=pltpu.CompilerParams(vmem_limit_bytes=VMEM_LIMIT),
    )(*results))


def solution(mesh):
    tokens = P(("grp", "ctx"), "tp")
    return jax.shard_map(
        local,
        mesh=mesh,
        in_specs=(tokens, tokens, tokens, P(("grp", "ctx", "tp"), None), P(None, "tp")),
        out_specs=(tokens, tokens, tokens, P(None, ("grp", "tp"))),
        check_vma=False,
    )
```

```python
import functools
import math

import jax
import jax.numpy as jnp
import ml_dtypes
import numpy as np
from jax import lax
from jax.experimental import pallas as pl
from jax.experimental.pallas import tpu as pltpu
from jax.sharding import PartitionSpec as P

MESH = pl.DeviceIdType.MESH
F32 = jnp.float32
BF16 = jnp.bfloat16
WIDTH = 512
CUTS = 4
VMEM_LIMIT = 60 * 1024 * 1024
DIRECT_PEERS = 8
PLAN = (
    "g0 g1 g2 g3 C0 h0 h1 C1 s0 M0 h2 h3 C2 s1 M1 L0 X0 C3 s2 s3 "
    "M2 L1 P0 X1 M3 L2 P1 X2 L3 P2 X3 P3 D0 D1 D2 D3"
)


def split(matrix):
    high = matrix.astype(ml_dtypes.bfloat16)
    low = (matrix - high.astype(np.float64)).astype(ml_dtypes.bfloat16)
    return np.concatenate([high, low], axis=0)


def transforms(length):
    half = length // 2
    turns = (2 * np.arange(half)[:, None] + 1) * np.arange(length)[None, :] % (2 * length)
    angle = np.pi * turns / length
    forward = np.concatenate([np.cos(angle), -np.sin(angle)], axis=0)
    inverse = forward.T / half
    return split(forward), split(inverse[:half]), split(inverse[half:])


def spectrum(matrix, rows):
    both = jnp.dot(matrix, rows, preferred_element_type=F32)
    half = both.shape[0] // 2
    return both[:half] + both[half:]


def restore(matrix, freqs):
    half = matrix.shape[0] // 2
    high = freqs.astype(BF16)
    low = (freqs - high.astype(F32)).astype(BF16)
    both = jnp.dot(matrix, high, preferred_element_type=F32)
    extra = jnp.dot(matrix[:half], low, preferred_element_type=F32)
    return both[:half] + both[half:] + extra


def times(a, b):
    half = a.shape[0] // 2
    ar, ai, br, bi = a[:half], a[half:], b[:half], b[half:]
    return jnp.concatenate([ar * br - ai * bi, ar * bi + ai * br], axis=0)


def times_conj(a, b):
    half = a.shape[0] // 2
    ar, ai, br, bi = a[:half], a[half:], b[:half], b[half:]
    return jnp.concatenate([ar * br + ai * bi, ai * br - ar * bi], axis=0)


def kernel(
    peers, direct, scale,
    q_hbm, k_hbm, v_hbm, og_hbm, h_hbm, fwd_hbm, inv0_hbm, inv1_hbm,
    dq_hbm, dk_hbm, dv_hbm, df_hbm,
    dq_ref, dk_ref, dv_ref, df_ref, q_ref, k_ref, v_ref, h_ref, fwd_ref, inv0_ref, inv1_ref,
    up, prod, gate, before, after, part, lane_in, pair_in, pair_out, hspec, pspecs,
    kv_sems, in_sems, up_sems, halo_send, halo_recv,
    lane_send, lane_recv, pair_send, pair_recv, ag_send, ag_recv, out_sems,
):
    grp, me, core = (lax.axis_index(a) for a in ("grp", "ctx", "tp"))
    rows, channels = q_ref.shape
    taps = h_ref.shape[0]
    chunks = channels // WIDTH
    mine = rows // 2
    has_before, has_after = me > 0, me < peers - 1
    lanes = max(peers // 2, 1)
    place, side = me // 2, lax.rem(me, 2)
    twin = 2 * place + 1 - side

    def at(other):
        return (grp, other, core)

    def lane(step):
        return 2 * lax.rem(place + step, lanes) + side

    after_me, before_me = lax.rem(me + 1, peers), lax.rem(me + peers - 1, peers)
    barrier = pltpu.get_barrier_semaphore()
    greeted = [(grp, me, 1 - core), at(after_me), at(before_me)]
    if direct:
        greeted += [at(lane(step)) for step in range(1, lanes)]
    for device in greeted:
        pl.semaphore_signal(barrier, inc=1, device_id=device, device_id_type=MESH)

    def columns(index):
        return pl.ds(index * WIDTH, WIDTH)

    kv_loads = []
    for index in range(chunks):
        cols = columns(index)
        kv_loads.append([
            pltpu.make_async_copy(hbm.at[:, cols], ref.at[:, cols], kv_sems.at[number, index])
            for number, (hbm, ref) in enumerate([(k_hbm, k_ref), (v_hbm, v_ref)])
        ])
        for copy in kv_loads[-1]:
            copy.start()
    own_rows = up.at[pl.ds(pl.multiple_of(core * mine, mine), mine)]
    near = og_hbm.at[:, pl.ds(pl.multiple_of(core * channels, channels), channels)]
    far = og_hbm.at[:, pl.ds(pl.multiple_of((1 - core) * channels, channels), channels)]
    others = [(q_hbm, q_ref), (h_hbm, h_ref), (fwd_hbm, fwd_ref), (inv0_hbm, inv0_ref),
              (inv1_hbm, inv1_ref), (near, own_rows)]
    loads = [pltpu.make_async_copy(hbm, ref, in_sems.at[number])
             for number, (hbm, ref) in enumerate(others)]
    for copy in loads:
        copy.start()

    up_copy = pltpu.make_async_remote_copy(
        src_ref=far, dst_ref=own_rows, send_sem=up_sems.at[0], recv_sem=up_sems.at[1],
        device_id=(grp, me, 1 - core), device_id_type=MESH,
    )

    def upward(index):
        return pltpu.make_async_remote_copy(
            src_ref=prod.at[index], dst_ref=before.at[index],
            send_sem=halo_send.at[0, index], recv_sem=halo_recv.at[0, index],
            device_id=at(after_me), device_id_type=MESH,
        )

    def downward(index):
        return pltpu.make_async_remote_copy(
            src_ref=gate.at[index], dst_ref=after.at[index],
            send_sem=halo_send.at[1, index], recv_sem=halo_recv.at[1, index],
            device_id=at(before_me), device_id_type=MESH,
        )

    share = taps // lanes if direct else taps

    near_lane = place + 1 - 2 * lax.rem(place, 2)
    far_block = lax.rem(place + 2, lanes)

    def scatter(step, index):
        owner = (near_lane, lax.rem(near_lane + 2, lanes), far_block)[step - 1]
        target = 2 * (near_lane if step < 3 else far_block) + side
        return pltpu.make_async_remote_copy(
            src_ref=part.at[index, pl.ds(pl.multiple_of(owner * share, share), share)],
            dst_ref=lane_in.at[step - 1, index],
            send_sem=lane_send.at[step - 1, index], recv_sem=lane_recv.at[step - 1, index],
            device_id=at(target), device_id_type=MESH,
        )

    def swap(index):
        return pltpu.make_async_remote_copy(
            src_ref=pair_out.at[index], dst_ref=pair_in.at[index],
            send_sem=pair_send.at[index], recv_sem=pair_recv.at[index],
            device_id=at(twin), device_id_type=MESH,
        )

    def block(step, index):
        holder = lax.rem(place + lanes - step, lanes)
        start = pl.multiple_of(holder * share, share)
        return df_ref.at[pl.ds(start, share), columns(index)]

    def collect(step, index):
        return pltpu.make_async_remote_copy(
            src_ref=block(0, index), dst_ref=block(0, index),
            send_sem=ag_send.at[step - 1, index], recv_sem=ag_recv.at[step - 1, index],
            device_id=at(lane(step)), device_id_type=MESH,
        )

    def store(number, index):
        ref = (dq_ref, dk_ref, dv_ref, df_ref)[number]
        hbm = (dq_hbm, dk_hbm, dv_hbm, df_hbm)[number]
        cols = columns(index)
        return pltpu.make_async_copy(ref.at[:, cols], hbm.at[:, cols], out_sems.at[number, index])

    def make_product(index):
        cols = columns(index)
        for copy in kv_loads[index]:
            copy.wait()
        prod[index] = (k_ref[:, cols].astype(F32) * v_ref[:, cols].astype(F32)).astype(BF16)

    make_product(0)
    pl.semaphore_wait(barrier, len(greeted))
    up_copy.start()
    for index in range(chunks):
        if index:
            make_product(index)

        @pl.when(has_after)
        def _():
            upward(index).start()

    for copy in loads:
        copy.wait()
    up_copy.wait()

    @pl.when(jnp.logical_not(has_before))
    def _():
        before[...] = jnp.zeros_like(before)

    @pl.when(jnp.logical_not(has_after))
    def _():
        after[...] = jnp.zeros_like(after)

    def make_gate(index):
        cols = columns(index)
        gate[index] = (up[:, cols].astype(F32) * q_ref[:, cols].astype(F32)).astype(BF16)

    def send_gate(index):
        @pl.when(has_before)
        def _():
            downward(index).start()

    def first(index):
        cols = columns(index)

        @pl.when(has_before)
        def _():
            upward(index).wait_recv()

        pspec = spectrum(fwd_ref[...], jnp.concatenate([before[index], prod[index]], axis=0))
        gspec = spectrum(fwd_ref[:, rows:], gate[index])
        terms = restore(inv0_ref[...], times_conj(gspec, pspec))
        if direct:
            part[index] = terms.astype(BF16)
            for step in (2, 1):
                scatter(step, index).start()
        else:
            df_ref[:, cols] = terms
            store(3, index).start()
        pspecs[index] = pspec

    def mix(index):
        cols = columns(index)
        mixture = restore(inv1_ref[...], times(pspecs[index], hspec[index]))
        dq_ref[:, cols] = (up[:, cols].astype(F32) * mixture).astype(BF16)
        store(0, index).start()

    def second(index):
        cols = columns(index)

        @pl.when(has_after)
        def _():
            downward(index).wait_recv()

        gspec = spectrum(fwd_ref[...], jnp.concatenate([gate[index], after[index]], axis=0))
        spread = restore(inv0_ref[...], times_conj(gspec, hspec[index]))
        dk_ref[:, cols] = (spread * v_ref[:, cols].astype(F32)).astype(BF16)
        dv_ref[:, cols] = (spread * k_ref[:, cols].astype(F32)).astype(BF16)
        store(1, index).start()
        store(2, index).start()

    def lane_total(index):
        own = pl.ds(pl.multiple_of(place * share, share), share)
        total = part[index, own].astype(F32)
        for slot in (0, 2):
            total = total + lane_in[slot, index].astype(F32)
        return total

    def halve(index):
        scatter(2, index).wait_recv()
        other = pl.ds(pl.multiple_of(far_block * share, share), share)
        total = part[index, other].astype(F32) + lane_in[1, index].astype(F32)
        part[index, other] = total.astype(BF16)
        scatter(3, index).start()

    def reduce_lane(index):
        for step in (1, 3):
            scatter(step, index).wait_recv()
        pair_out[index] = lane_total(index).astype(BF16)
        swap(index).start()

    def reduce_pair(index):
        swap(index).wait_recv()
        total = pair_out[index].astype(F32) + pair_in[index].astype(F32)
        block(0, index)[...] = (total * scale).astype(BF16)
        for step in range(1, lanes):
            collect(step, index).start()

    def taps_spectrum(index):
        hspec[index] = spectrum(fwd_ref[:, :taps], h_ref[:, columns(index)])

    run = dict(g=make_gate, s=send_gate, h=taps_spectrum, C=first, X=mix, D=second)
    if direct:
        run.update(M=halve, L=reduce_lane, P=reduce_pair)
    for entry in PLAN.split():
        if entry[0] in run:
            run[entry[0]](int(entry[1]))

    for index in range(chunks):
        @pl.when(has_after)
        def _():
            upward(index).wait_send()

        @pl.when(has_before)
        def _():
            downward(index).wait_send()

        if direct:
            for step in range(1, lanes):
                scatter(step, index).wait_send()
                collect(step, index).wait()
            swap(index).wait_send()
            store(3, index).start()
    for index in range(chunks):
        for number in range(4):
            store(number, index).wait()


def deliver(*refs):
    count = len(refs) // 3
    sources, targets, held, sems = refs[:count], refs[count:2 * count], refs[2 * count:-1], refs[-1]
    loads, stores = [], []
    for i in range(count):
        rows = sources[i].shape[0] // CUTS
        for j in range(CUTS):
            part = pl.ds(j * rows, rows)
            here = held[i].at[part]
            loads.append(pltpu.make_async_copy(sources[i].at[part], here, sems.at[0, i, j]))
            stores.append(pltpu.make_async_copy(here, targets[i].at[part], sems.at[1, i, j]))
    for load in loads:
        load.start()
    for load, store in zip(loads, stores):
        load.wait()
        store.start()
    for store in stores:
        store.wait()


def local(queries, key_proj, value_proj, out_grad, filter_taps):
    rows, channels = queries.shape
    taps = filter_taps.shape[0]
    peers = lax.axis_size("ctx")
    direct = peers == DIRECT_PEERS
    scale = 1.0 / math.sqrt(peers * rows)
    chunks = channels // WIDTH
    matrices = [jnp.asarray(m) for m in transforms(2 * rows)]
    lanes = peers // 2 if direct else 2
    share = taps // lanes if direct else 32
    like = jax.ShapeDtypeStruct((rows, channels), BF16)
    hbm = pl.BlockSpec(memory_space=pltpu.HBM)
    tile = (chunks, rows, WIDTH)
    dma = pltpu.SemaphoreType.DMA
    whole = [pltpu.VMEM(x.shape, BF16)
             for x in (queries, key_proj, value_proj, filter_taps, *matrices)]
    results = pl.pallas_call(
        functools.partial(kernel, peers, direct, scale),
        name="hyena_backward",
        out_shape=[like, like, like,
                   jax.ShapeDtypeStruct((taps, channels), BF16 if direct else F32)],
        in_specs=[hbm] * 8,
        out_specs=[hbm] * 4,
        scratch_shapes=[pltpu.VMEM((rows, channels), BF16)] * 3
        + [pltpu.VMEM((taps, channels), BF16 if direct else F32)] + whole + [pltpu.VMEM((rows, channels), BF16)]
        + [pltpu.VMEM(tile, BF16)] * 4 + [
            pltpu.VMEM((chunks, taps, WIDTH), BF16),
            pltpu.VMEM((lanes - 1, chunks, share, WIDTH), BF16),
            pltpu.VMEM((chunks, share, WIDTH), BF16),
            pltpu.VMEM((chunks, share, WIDTH), BF16),
            pltpu.VMEM((chunks, 2 * rows, WIDTH), F32),
            pltpu.VMEM((chunks, 2 * rows, WIDTH), F32),
            dma((2, chunks)), dma((6,)), dma((2,)), dma((2, chunks)), dma((2, chunks)),
            dma((lanes - 1, chunks)), dma((lanes - 1, chunks)), dma((chunks,)), dma((chunks,)),
            dma((lanes - 1, chunks)), dma((lanes - 1, chunks)),
            dma((4, chunks)),
        ],
        compiler_params=pltpu.CompilerParams(
            collective_id=0, has_side_effects=True, vmem_limit_bytes=VMEM_LIMIT
        ),
        cost_estimate=pl.CostEstimate(
            flops=20 * rows * rows * channels, bytes_accessed=18 * rows * channels,
            transcendentals=0,
        ),
    )(queries, key_proj, value_proj, out_grad, filter_taps, *matrices)
    results = list(results)
    if not direct:
        results[3] = (lax.psum(results[3], "ctx") * scale).astype(BF16)
    return tuple(pl.pallas_call(
        deliver,
        name="deliver",
        out_shape=[jax.ShapeDtypeStruct(x.shape, x.dtype) for x in results],
        in_specs=[hbm] * 4,
        out_specs=[hbm] * 4,
        scratch_shapes=[pltpu.VMEM(x.shape, x.dtype) for x in results] + [dma((2, 4, CUTS))],
        compiler_params=pltpu.CompilerParams(vmem_limit_bytes=VMEM_LIMIT),
    )(*results))


def solution(mesh):
    tokens = P(("grp", "ctx"), "tp")
    return jax.shard_map(
        local,
        mesh=mesh,
        in_specs=(tokens, tokens, tokens, P(("grp", "ctx", "tp"), None), P(None, "tp")),
        out_specs=(tokens, tokens, tokens, P(None, ("grp", "tp"))),
        check_vma=False,
    )
```
